512 devices in a mesh: tok: 32 (over y_hi, z), head: 16 (over x, y_lo, core).
Axes of the slice: x: 4, y: 8 (y_hi: 4, y_lo: 2; y = y_hi * 2 + y_lo), z: 8, core: 2. Of those that a mesh axis runs over, the one named last changes fastest.
Arguments:
- queries: bfloat16 [1024, 12288], P('head', 'tok'), may hold values from -8 to 8
- keys: bfloat16 [1024, 12288], P('head', 'tok'), may hold values from -8 to 8
- values: bfloat16 [1024, 12288], P('head', 'tok'), may hold values from -6 to 6
- out_grad: bfloat16 [1024, 12288], P('head', 'tok'), may hold values from -6 to 6
- w_out: bfloat16 [1024, 1024], P('head'), may hold values from -0.1875 to 0.1875
- counts: int32 [32], P('tok'), may hold values from 48 to 384, as said below
- keep: int32 [12288], P('tok'), may hold values 0 or 1
Outputs:
- dq: bfloat16 [1024, 12288], P('head', 'tok')
- dk: bfloat16 [1024, 12288], P('head', 'tok')
- dv: bfloat16 [1024, 12288], P('head', 'tok')
- d_wout: float32 [1024, 1024], P('head')
The draws below stay inside these ranges and needn't reach their ends.
Inputs may be any that keep to these rules, and one draw needn't show every extreme that they name: The valid tokens of a block are its first counts entries; some block is full, and some block holds exactly 48.
All inputs are finite; a program needn't handle non-finite values. No bound on the sum of `keep` on one device may be relied on, other than what follows from the above.
Results may differ from the reference program's by a relative error of at most 0.04.
Values may be sent and summed in bfloat16 or wider, within the bound.
No kernel may reach another device: no remote copies, remote signals or barrier semaphores. Data moves between devices by JAX's collectives and lax.ppermute only.
A program may use at most 64 MiB of HBM per device.

```python
import math
import jax
import jax.numpy as jnp
from jax import lax

D = 1024
HEADS = 16
HD = 64
TOK_DEV = 384
TOKENS = 12288


def draw_queries(key, part):
    key = jax.random.fold_in(key, 3)
    drawn = jnp.clip(1.4 * jax.random.normal(key, (D, TOKENS), jnp.float32), -8.0, 8.0)
    return drawn.astype(jnp.bfloat16)


def draw_keys(key, part):
    key = jax.random.fold_in(key, 5)
    drawn = jnp.clip(1.4 * jax.random.normal(key, (D, TOKENS), jnp.float32), -8.0, 8.0)
    return drawn.astype(jnp.bfloat16)


def draw_counts(key, part):
    key = jax.random.fold_in(key, 21)
    shards = TOKENS // TOK_DEV
    lowest = TOK_DEV // 8
    draws = jax.random.randint(jax.random.fold_in(key, 1), (shards,), 0, 64)
    drawn = lowest + (TOK_DEV - lowest) * draws * draws // 3969
    full = jax.random.randint(jax.random.fold_in(key, 2), (), 0, shards)
    small = (full + 1 + jax.random.randint(jax.random.fold_in(key, 3), (), 0, shards - 1)) % shards
    drawn = drawn.at[full].set(TOK_DEV).at[small].set(lowest)
    return drawn.astype(jnp.int32)


def with_ends(result, rng, least, top_value):
    place = [jax.random.randint(jax.random.fold_in(rng, axis), (), 0, length) for axis, length in enumerate(result.shape)]
    main_axis = result.shape.index(max(result.shape))
    beside = place[:main_axis] + [(place[main_axis] + 1) % result.shape[main_axis]] + place[main_axis + 1:]
    return result.at[tuple(place)].set(least).at[tuple(beside)].set(top_value)


def block_scale(key, extent, split, smallest, top_value):
    def one(position, parts):
        steps = jax.random.uniform(jax.random.fold_in(jax.random.fold_in(key, 6), position), (parts,), jnp.float32, smallest / len(split), top_value / len(split))
        return jnp.repeat(jnp.exp(steps), extent[position] // parts).reshape((-1,) + (1,) * (len(extent) - position - 1))

    factor_of = one(*split[0])
    for cut in split[1:]:
        factor_of = factor_of * one(*cut)
    return factor_of


def normal_values(key, shape, deviation, bound, split=(), held_as=jnp.bfloat16):
    result = jax.random.normal(key, shape, jnp.float32) * deviation
    if len(split) > 0:
        result = block_scale(key, shape, split, -0.22, 0.18) * result
    return jnp.clip(result, min=-bound, max=bound).astype(held_as)


def setup_inputs(seed: int = 0) -> dict:
    streams_of = jax.random.split(jax.random.key(seed), 8)
    queries = draw_queries(jax.random.fold_in(streams_of[7], 71), 0)
    keys = draw_keys(jax.random.fold_in(streams_of[7], 71), 0)
    values = normal_values(streams_of[2], (D, TOKENS), 1.0, 6.0, ((0, 16), (1, 32)))
    out_grad = normal_values(streams_of[3], (D, TOKENS), 1.0, 6.0, ((0, 16), (1, 32)))
    w_out = normal_values(streams_of[4], (D, D), D ** -0.5, 0.1875, ((0, 16),))
    counts = draw_counts(jax.random.fold_in(streams_of[7], 71), 0)
    keep = with_ends((jax.random.randint(streams_of[6], (TOKENS,), 0, 4) < 3).astype(jnp.int32), jax.random.fold_in(streams_of[6], 1), 0, 1)
    return {"queries": queries, "keys": keys, "values": values, "out_grad": out_grad, "w_out": w_out, "counts": counts, "keep": keep}


NEGATIVE_FILL = -1e+30

def reference(queries, keys, values, out_grad, w_out, counts, keep):
    scale = 1.0 / math.sqrt(HD)
    pos = jnp.arange(TOKENS, dtype=jnp.int32)
    shard = pos // TOK_DEV
    valid_entries = pos - shard * TOK_DEV < jnp.take(counts, shard)
    live = jnp.where(valid_entries, keep, 0).astype(jnp.bfloat16)
    grad = out_grad * live[None, :]
    d_attn_all = jnp.dot(w_out, grad, preferred_element_type=jnp.float32).astype(jnp.bfloat16)
    blocks = TOKENS // TOK_DEV
    valid_key_mask = valid_entries[None, :]

    def one_head(head):
        rows = (head * HD).astype(jnp.int32)
        qh = lax.dynamic_slice_in_dim(queries, rows, HD, 0)
        kh = lax.dynamic_slice_in_dim(keys, rows, HD, 0)
        vh = lax.dynamic_slice_in_dim(values, rows, HD, 0)
        vh_wide = vh.astype(jnp.float32)
        dh = lax.dynamic_slice_in_dim(d_attn_all, rows, HD, 0)

        def step(carry, index):
            dk_acc, dv_acc = carry
            start = (index * TOK_DEV).astype(jnp.int32)
            qb = lax.dynamic_slice_in_dim(qh, start, TOK_DEV, 1)
            db = lax.dynamic_slice_in_dim(dh, start, TOK_DEV, 1)
            score_matrix = lax.dot_general(qb, kh, (((0,), (0,)), ((), ())), preferred_element_type=jnp.float32) * scale
            score_matrix = jnp.where(valid_key_mask, score_matrix, NEGATIVE_FILL)
            running_maximum = lax.optimization_barrier(jnp.max(score_matrix, axis=1, keepdims=True))
            exponent_terms = jnp.where(valid_key_mask, jnp.exp(score_matrix - running_maximum), 0.0)
            total = lax.optimization_barrier(jnp.sum(exponent_terms, axis=1))
            attn = lax.dot_general(exponent_terms, vh_wide, (((1,), (1,)), ((), ())), precision=lax.Precision.HIGHEST, preferred_element_type=jnp.float32)
            attn = (attn / total[:, None]).astype(jnp.bfloat16)
            log_sum_exponent = running_maximum[:, 0] + jnp.log(total)
            delta = lax.optimization_barrier(jnp.sum(db.astype(jnp.float32) * attn.T.astype(jnp.float32), axis=0))
            probability_rows = jnp.where(valid_key_mask, jnp.exp(score_matrix - log_sum_exponent[:, None]), 0.0)
            dprob = lax.dot_general(db, vh, (((0,), (0,)), ((), ())), preferred_element_type=jnp.float32)
            dscore = probability_rows * (dprob - delta[:, None])
            dscore_low = dscore.astype(jnp.bfloat16)
            prob_low = probability_rows.astype(jnp.bfloat16)
            dq_b = lax.dot_general(kh, dscore_low, (((1,), (1,)), ((), ())), preferred_element_type=jnp.float32)
            dq_b = (scale * dq_b).astype(jnp.bfloat16)
            dk_acc = dk_acc + lax.dot_general(qb, dscore_low, (((1,), (0,)), ((), ())), preferred_element_type=jnp.float32)
            dv_acc = dv_acc + lax.dot_general(db, prob_low, (((1,), (0,)), ((), ())), preferred_element_type=jnp.float32)
            return ((dk_acc, dv_acc), (attn, dq_b))
        zero = jnp.zeros((HD, TOKENS), jnp.float32)
        (dk_acc, dv_acc), (attn_blocks, dq_blocks) = lax.scan(step, (zero, zero), jnp.arange(blocks, dtype=jnp.int32))
        attn_all = attn_blocks.reshape(TOKENS, HD)
        dq_h = jnp.transpose(dq_blocks, (1, 0, 2)).reshape(HD, TOKENS)
        dw_h = lax.dot_general(attn_all, grad, (((0,), (1,)), ((), ())), preferred_element_type=jnp.float32)
        return (dq_h, (scale * dk_acc).astype(jnp.bfloat16), dv_acc.astype(jnp.bfloat16), dw_h)
    dq_all, dk_all, dv_all, dw_all = lax.map(one_head, jnp.arange(HEADS, dtype=jnp.int32))
    return (dq_all.reshape(D, TOKENS), dk_all.reshape(D, TOKENS), dv_all.reshape(D, TOKENS), dw_all.reshape(D, D))
```

```python
import jax
import jax.numpy as jnp
from jax import lax
from jax.experimental import pallas as pl
from jax.experimental.pallas import tpu as pltpu
from jax.sharding import PartitionSpec as P

HD = 64
TB = 384
NY = 4
NZ = 8
CH = 128
NCH = TB // CH
TK = 256
TQ = 256
KROWS = NZ * TB
QCOLS = NY * TB
EXT = 16
BIAS = -30000.0
BF = jnp.bfloat16
F32 = jnp.float32
Z_GROUPS = [[y * NZ + z for z in range(NZ)] for y in range(NY)]
Y_GROUPS = [[y * NZ + z for y in range(NY)] for z in range(NZ)]


def dot(a, b):
    return jnp.dot(a, b, preferred_element_type=F32)


def dot_nt(a, b):
    return lax.dot_general(a, b, (((1,), (1,)), ((), ())), preferred_element_type=F32)


def pieces(x):
    hi = x.astype(BF)
    rest = x - hi.astype(F32)
    mid = rest.astype(BF)
    low = (rest - mid.astype(F32)).astype(BF)
    return hi, mid, low


def count_of(meta):
    meta = meta.astype(F32)
    return jnp.max(meta[0:1, 0:CH] * 16.0 + meta[1:2, 0:CH]).astype(jnp.int32)


def pack_keys(kv_ref, kvp_ref):
    lane = lax.broadcasted_iota(jnp.int32, (TB, CH), 1)
    row = lax.broadcasted_iota(jnp.int32, (TB, CH), 0)
    ones = jnp.where((lane >= 1) & (lane <= 3), 1.0, 0.0)
    offset = jnp.int32(0)
    offsets = []
    for b in range(NZ):
        cnt = count_of(kv_ref[b, TB : TB + EXT, :])
        here = pl.multiple_of(offset, 16)
        kvp_ref[pl.ds(here, TB), 0:CH] = kv_ref[b, 0:TB, :]
        aux = jnp.where((lane == 0) & (row >= cnt), BIAS, ones)
        kvp_ref[pl.ds(here, TB), CH : 2 * CH] = aux.astype(BF)
        size = ((cnt + 15) // 16) * 16
        offsets.append((here, size))
        offset = offset + size
    here = pl.multiple_of(offset, 16)
    kvp_ref[pl.ds(here, TK), 0:CH] = jnp.zeros((TK, CH), BF)
    tail = jnp.where(lane[0:TK] == 0, BIAS, ones[0:TK])
    kvp_ref[pl.ds(here, TK), CH : 2 * CH] = tail.astype(BF)
    return offsets, (offset + TK - 1) // TK


def eye(n):
    r = lax.broadcasted_iota(jnp.int32, (n, n), 0)
    c = lax.broadcasted_iota(jnp.int32, (n, n), 1)
    return jnp.where(r == c, 1.0, 0.0).astype(BF)


def transpose_keys(kvp_ref, kvt_ref, n_key_tiles):
    unit = eye(CH)

    def one(kt, _):
        at = pl.multiple_of(kt * TK, TK)
        kvt_ref[:, pl.ds(at, TK)] = dot_nt(unit, kvp_ref[pl.ds(at, TK), 0:CH]).astype(BF)
        return 0

    lax.fori_loop(0, n_key_tiles, one, 0)


def query_chunks(x_ref):
    n = jnp.int32(0)
    chunks = []
    for b in range(NY):
        cnt = count_of(x_ref[b, 2 * HD : 2 * HD + EXT, :])
        for c in range(NCH):
            active = cnt > c * CH
            chunks.append((b, c, active, pl.multiple_of(n * CH, CH)))
            n = n + active.astype(jnp.int32)
    return chunks, (n * CH + TQ - 1) // TQ


def pack_queries(x_ref, ws_ref, wd_ref, chunks):
    ws_ref[...] = jnp.zeros(ws_ref.shape, BF)
    wd_ref[...] = jnp.zeros(wd_ref.shape, BF)
    first = lax.broadcasted_iota(jnp.int32, (EXT, QCOLS + CH), 0) == 0
    ws_ref[CH : CH + EXT, :] = jnp.where(first, 1.0, 0.0).astype(BF)
    for b, c, active, at in chunks:
        @pl.when(active)
        def _():
            part = slice(c * CH, (c + 1) * CH)
            ws_ref[0:HD, pl.ds(at, CH)] = x_ref[b, 0:HD, part]
            wd_ref[HD : 2 * HD, pl.ds(at, CH)] = x_ref[b, HD : 2 * HD, part]


def forward_kernel(kv_ref, x_ref, out_ref, kvp_ref, kvt_ref, ws_ref, wd_ref, acc_ref, st_ref, stu_ref):
    _, n_key_tiles = pack_keys(kv_ref, kvp_ref)
    transpose_keys(kvp_ref, kvt_ref, n_key_tiles)
    chunks, n_query_tiles = query_chunks(x_ref)
    pack_queries(x_ref, ws_ref, wd_ref, chunks)

    def query_tile(qt, _):
        q0 = pl.multiple_of(qt * TQ, TQ)
        ws = ws_ref[:, pl.ds(q0, TQ)]
        wd = wd_ref[:, pl.ds(q0, TQ)]

        def key_tile(kt, carry):
            top, total, dsum, acc = carry
            k0 = pl.multiple_of(kt * TK, TK)
            kv = kvp_ref[pl.ds(k0, TK), :]
            s = dot(kv, ws)
            dp = dot(kv, wd)
            new = jnp.maximum(top, jnp.max(s, axis=0, keepdims=True))
            e = jnp.exp(s - new)
            fade = jnp.exp(top - new)
            total = total * fade + jnp.sum(e, axis=0, keepdims=True)
            dsum = dsum * fade + jnp.sum(e * dp, axis=0, keepdims=True)
            acc = acc * fade + dot(kvt_ref[HD : 2 * HD, pl.ds(k0, TK)], e.astype(BF))
            return new, total, dsum, acc

        zero = jnp.zeros((1, TQ), F32)
        top, total, dsum, acc = lax.fori_loop(
            0, n_key_tiles, key_tile, (zero - 1e30, zero, zero, jnp.zeros((HD, TQ), F32))
        )
        acc_ref[:, pl.ds(q0, TQ)] = acc / total
        st_ref[0:1, pl.ds(q0, TQ)] = top
        st_ref[1:2, pl.ds(q0, TQ)] = total
        st_ref[2:3, pl.ds(q0, TQ)] = dsum
        return 0

    lax.fori_loop(0, n_query_tiles, query_tile, 0)

    row = lax.broadcasted_iota(jnp.int32, (EXT, TB), 0)
    stu_ref[...] = jnp.where((row >= NY) & (row < 2 * NY), 1.0, 0.0)
    out_ref[...] = jnp.zeros(out_ref.shape, BF)
    for b, c, active, at in chunks:
        @pl.when(active)
        def _():
            part = slice(c * CH, (c + 1) * CH)
            out_ref[b, 0:HD, part] = acc_ref[:, pl.ds(at, CH)].astype(BF)
            for i in range(3):
                stu_ref[i * NY + b : i * NY + b + 1, part] = st_ref[i : i + 1, pl.ds(at, CH)]
    split = pieces(stu_ref[...])
    for b in range(NY):
        for i in range(3):
            out_ref[b, HD + i * EXT : HD + (i + 1) * EXT, :] = split[i]


def merged_stats(r_ref):
    stats = []
    for s in range(NY):
        st = r_ref[s, HD : HD + EXT, :].astype(F32)
        st = st + r_ref[s, HD + EXT : HD + 2 * EXT, :].astype(F32)
        stats.append(st + r_ref[s, HD + 2 * EXT : HD + 3 * EXT, :].astype(F32))
    top = stats[0][0:NY]
    for s in range(1, NY):
        top = jnp.maximum(top, stats[s][0:NY])
    shares = []
    total = jnp.zeros((NY, TB), F32)
    dsum = jnp.zeros((NY, TB), F32)
    for s in range(NY):
        fade = jnp.exp(stats[s][0:NY] - top)
        shares.append(stats[s][NY : 2 * NY] * fade)
        total = total + shares[s]
        dsum = dsum + stats[s][2 * NY : 3 * NY] * fade
    return top + jnp.log(total), dsum / total, [share / total for share in shares]


def combine_kernel(y_ref, r_ref, grad_ref, out_ref, share_ref):
    _, _, shares = merged_stats(r_ref)
    for s in range(NY):
        share_ref[s] = shares[s]
    own = y_ref[0]
    attn = jnp.zeros((HD, TB), F32)
    for s in range(NY):
        attn = attn + r_ref[s, 0:HD, :].astype(F32) * share_ref[s, pl.ds(own, 1), :]
    attn = attn.astype(BF)
    for z in range(NZ):
        part = dot_nt(attn, grad_ref[z * CH : (z + 1) * CH, :])
        for y in range(NY):
            out_ref[y * NZ + z] = part[y * 16 : (y + 1) * 16, :].astype(BF)


def backward_kernel(
    kv_ref, x_ref, r_ref, dq_ref, dkv_ref, kvp_ref, kvt_ref, ws_ref, wd_ref, xq_ref, xd_ref, lse_ref, dl_ref, dqa_ref, dkva_ref
):
    offsets, n_key_tiles = pack_keys(kv_ref, kvp_ref)
    transpose_keys(kvp_ref, kvt_ref, n_key_tiles)
    chunks, n_query_tiles = query_chunks(x_ref)
    pack_queries(x_ref, ws_ref, wd_ref, chunks)
    lse, delta, _ = merged_stats(r_ref)
    for i, piece in enumerate(pieces(-lse)):
        lse_ref[i] = piece.astype(F32)
    for i, piece in enumerate(pieces(-delta)):
        dl_ref[i] = piece.astype(F32)
    row = lax.broadcasted_iota(jnp.int32, (EXT, CH), 0)
    for b, c, active, at in chunks:
        @pl.when(active)
        def _():
            part = slice(c * CH, (c + 1) * CH)
            tile_s = jnp.where(row == 0, 1.0, 0.0)
            tile_d = jnp.zeros((EXT, CH), F32)
            for i in range(3):
                tile_s = jnp.where(row == i + 1, lse_ref[i, b : b + 1, part], tile_s)
                tile_d = jnp.where(row == i + 1, dl_ref[i, b : b + 1, part], tile_d)
            ws_ref[CH : CH + EXT, pl.ds(at, CH)] = tile_s.astype(BF)
            wd_ref[CH : CH + EXT, pl.ds(at, CH)] = tile_d.astype(BF)

    unit = eye(TQ)

    def turn(qt, _):
        q0 = pl.multiple_of(qt * TQ, TQ)
        xq_ref[pl.ds(q0, TQ), :] = dot_nt(unit, ws_ref[0:CH, pl.ds(q0, TQ)]).astype(BF)
        xd_ref[pl.ds(q0, TQ), :] = dot_nt(unit, wd_ref[0:CH, pl.ds(q0, TQ)]).astype(BF)
        return 0

    lax.fori_loop(0, n_query_tiles, turn, 0)
    dqa_ref[...] = jnp.zeros(dqa_ref.shape, F32)

    def key_tile(kt, _):
        k0 = pl.multiple_of(kt * TK, TK)
        kv = kvp_ref[pl.ds(k0, TK), :]
        kt_rows = kvt_ref[0:HD, pl.ds(k0, TK)]

        def query_tile(qt, acc):
            q0 = pl.multiple_of(qt * TQ, TQ)
            prob = jnp.exp(dot(kv, ws_ref[:, pl.ds(q0, TQ)]))
            dscore = (prob * dot(kv, wd_ref[:, pl.ds(q0, TQ)])).astype(BF)
            prob = prob.astype(BF)
            dqa_ref[:, pl.ds(q0, TQ)] += dot(kt_rows, dscore)
            acc = acc + dot(dscore, xq_ref[pl.ds(q0, TQ), :])
            return acc + dot(prob, xd_ref[pl.ds(q0, TQ), :])

        dkva_ref[pl.ds(k0, TK), :] = lax.fori_loop(0, n_query_tiles, query_tile, jnp.zeros((TK, CH), F32))
        return 0

    lax.fori_loop(0, n_key_tiles, key_tile, 0)

    dq_ref[...] = jnp.zeros(dq_ref.shape, BF)
    for b, c, active, at in chunks:
        @pl.when(active)
        def _():
            dq_ref[b, c * HD : (c + 1) * HD, :] = (0.125 * dqa_ref[:, pl.ds(at, CH)]).astype(BF)
    krow = lax.broadcasted_iota(jnp.int32, (TB, CH), 0)
    for b in range(NZ):
        here, size = offsets[b]
        got = dkva_ref[pl.ds(here, TB), :]
        dkv_ref[b, 0:TB, :] = jnp.where(krow < size, got, 0.0).astype(BF)
        dkv_ref[b, TB : TB + EXT, :] = jnp.zeros((EXT, CH), BF)


VMEM = pl.BlockSpec(memory_space=pltpu.VMEM)
SMEM = pl.BlockSpec(memory_space=pltpu.SMEM)
PARAMS = pltpu.CompilerParams(vmem_limit_bytes=48 * 1024 * 1024)


def packed_scratch():
    return [
        pltpu.VMEM((KROWS + TB, 2 * CH), BF),
        pltpu.VMEM((CH, KROWS + TK), BF),
        pltpu.VMEM((2 * CH, QCOLS + CH), BF),
        pltpu.VMEM((2 * CH, QCOLS + CH), BF),
    ]


def forward(kv_all, x_all):
    return pl.pallas_call(
        forward_kernel,
        out_shape=jax.ShapeDtypeStruct((NY, HD + 3 * EXT, TB), BF),
        in_specs=[VMEM, VMEM],
        out_specs=VMEM,
        scratch_shapes=packed_scratch()
        + [
            pltpu.VMEM((HD, QCOLS + CH), F32),
            pltpu.VMEM((8, QCOLS + CH), F32),
            pltpu.VMEM((EXT, TB), F32),
        ],
        compiler_params=PARAMS,
        cost_estimate=pl.CostEstimate(flops=4 * 10**9, bytes_accessed=2 * 10**6, transcendentals=0),
        name="forward",
    )(kv_all, x_all)


def combine(own, got, grad_all):
    return pl.pallas_call(
        combine_kernel,
        out_shape=jax.ShapeDtypeStruct((NY * NZ, 16, CH), BF),
        in_specs=[SMEM, VMEM, VMEM],
        out_specs=VMEM,
        scratch_shapes=[pltpu.VMEM((NY, NY, TB), F32)],
        compiler_params=PARAMS,
        cost_estimate=pl.CostEstimate(flops=5 * 10**7, bytes_accessed=2 * 10**6, transcendentals=0),
        name="combine",
    )(own, got, grad_all)


def backward(kv_all, x_all, got):
    return pl.pallas_call(
        backward_kernel,
        out_shape=(
            jax.ShapeDtypeStruct((NY, NCH * HD, CH), BF),
            jax.ShapeDtypeStruct((NZ, TB + EXT, CH), BF),
        ),
        in_specs=[VMEM, VMEM, VMEM],
        out_specs=(VMEM, VMEM),
        scratch_shapes=packed_scratch()
        + [
            pltpu.VMEM((QCOLS + CH, CH), BF),
            pltpu.VMEM((QCOLS + CH, CH), BF),
            pltpu.VMEM((3, NY, TB), F32),
            pltpu.VMEM((3, NY, TB), F32),
            pltpu.VMEM((HD, QCOLS + CH), F32),
            pltpu.VMEM((KROWS + TB, CH), F32),
        ],
        compiler_params=PARAMS,
        cost_estimate=pl.CostEstimate(flops=8 * 10**9, bytes_accessed=2 * 10**6, transcendentals=0),
        name="backward",
    )(kv_all, x_all, got)


def exchange(slots, axis, groups=None):
    return lax.all_to_all(slots, axis, 0, 0, tiled=True, axis_index_groups=groups)


def spread(block, count):
    return jnp.broadcast_to(block[None], (count,) + block.shape)


def on_device(queries, keys, values, out_grad, w_out, counts, keep):
    count = counts[0]
    valid = jnp.arange(TB, dtype=jnp.int32) < count
    live = jnp.where(valid, keep, 0).astype(BF)
    grad = out_grad * live[None, :]
    step = lax.broadcasted_iota(jnp.int32, (EXT, TB), 0)
    meta = jnp.where(step == 0, count // 16, jnp.where(step == 1, count % 16, 0)).astype(BF)
    kv = jnp.concatenate([jnp.concatenate([keys, values], 0).T, meta[:, 0:CH]], 0)
    kv_all = lax.all_gather(kv, "tok", axis=0, axis_index_groups=Z_GROUPS)
    grad_all = exchange(spread(grad, 16), "head").reshape(16 * HD, TB)
    d_attn = jnp.dot(w_out, grad_all, preferred_element_type=F32).astype(BF)
    x = jnp.concatenate([queries * jnp.asarray(0.125, BF), d_attn, meta], 0)
    x_all = exchange(spread(x, NY), "tok", Y_GROUPS)
    got = exchange(forward(kv_all, x_all), "tok", Y_GROUPS)
    own = (lax.axis_index("tok") // NZ).astype(jnp.int32).reshape(1)
    parts = exchange(combine(own, got, grad_all), "tok")
    dq_parts, dkv_parts = backward(kv_all, x_all, got)
    piece = jnp.sum(parts.astype(F32), axis=0).astype(BF)
    dkv_parts = dkv_parts.at[:, TB:, :].set(piece[None])
    dkv_got = exchange(dkv_parts, "tok", Z_GROUPS)
    row_pieces = dkv_got[:, TB:, :].reshape(NZ * 16, CH)
    last = jnp.concatenate([dq_parts, spread(row_pieces, NY)], 1)
    last = exchange(last, "tok", Y_GROUPS)
    dkv = jnp.sum(dkv_got[:, 0:TB, :].astype(F32), axis=0).astype(BF).T
    dq = jnp.sum(last[:, 0 : NCH * HD].astype(F32), axis=0).astype(BF)
    dq = dq.reshape(NCH, HD, CH).transpose(1, 0, 2).reshape(HD, TB)
    d_wout = last[:, NCH * HD :].reshape(NY, NZ, 16, CH).transpose(0, 2, 1, 3).reshape(HD, 16 * HD)
    return dq, dkv[0:HD], dkv[HD:], d_wout.astype(F32)


def solution(mesh):
    return jax.shard_map(
        on_device,
        mesh=mesh,
        in_specs=(
            P("head", "tok"),
            P("head", "tok"),
            P("head", "tok"),
            P("head", "tok"),
            P("head", None),
            P("tok"),
            P("tok"),
        ),
        out_specs=(P("head", "tok"), P("head", "tok"), P("head", "tok"), P("head", None)),
        check_vma=False,
    )
```

```python
import jax
import jax.numpy as jnp
from jax import lax
from jax.experimental import pallas as pl
from jax.experimental.pallas import tpu as pltpu
from jax.sharding import PartitionSpec as P

HD = 64
D = 1024
TB = 384
NY = 4
NZ = 8
CH = 128
NCH = TB // CH
TK = 256
TQ = 256
KROWS = NZ * TB
QCOLS = NY * TB
KPAD = KROWS + TB
QPAD = QCOLS + CH
WIDE = TB + CH
EXT = 16
BIAS = -30000.0
BF = jnp.bfloat16
F32 = jnp.float32
Z_GROUPS = [[y * NZ + z for z in range(NZ)] for y in range(NY)]
Y_GROUPS = [[y * NZ + z for y in range(NY)] for z in range(NZ)]
KEY_AT, KEY_SIZE, QUERY_AT, QUERY_SIZE, KEY_TILES, QUERY_TILES = 0, 8, 16, 20, 24, 25


def dot(a, b):
    return jnp.dot(a, b, preferred_element_type=F32)


def dot_nt(a, b):
    return lax.dot_general(a, b, (((1,), (1,)), ((), ())), preferred_element_type=F32)


def iota(shape, dim):
    return lax.broadcasted_iota(jnp.int32, shape, dim)


def eye(n):
    return jnp.where(iota((n, n), 0) == iota((n, n), 1), 1.0, 0.0).astype(BF)


def pieces(x):
    hi = x.astype(BF)
    rest = x - hi.astype(F32)
    mid = rest.astype(BF)
    low = (rest - mid.astype(F32)).astype(BF)
    return hi, mid, low


def two_rows(shape, first, second):
    row = iota(shape, 0)
    return jnp.where(row == 0, first, jnp.where(row == 1, second, 0.0)).astype(BF)


def count_of(meta):
    meta = meta.astype(F32)
    return jnp.max(meta[0:1, 0:CH] * 16.0 + meta[1:2, 0:CH]).astype(jnp.int32)


def place_matrix(spot):
    return jnp.where(iota((TB, TB), 0).astype(F32) == spot, 1.0, 0.0).astype(BF)


def prepare_kernel(count_ref, keys_ref, values_ref, out_grad_ref, keep_ref, kv_ref, grad_ref, spot_ref):
    count = count_ref[0]
    live = jnp.where(iota((8, TB), 1) < count, keep_ref[...].astype(F32), 0.0)
    grad_ref[...] = out_grad_ref[...] * live[0:1].astype(BF)
    upto = jnp.where(iota((TB, TB), 0) <= iota((TB, TB), 1), 1.0, 0.0).astype(BF)
    order = dot(live.astype(BF), upto)
    spot_ref[...] = jnp.where(live > 0.0, order - 1.0, -1.0)
    both = jnp.concatenate([keys_ref[...], values_ref[...]], 0)
    turned = dot_nt(eye(TB), both).astype(BF)
    high = (count // 16).astype(F32)
    low = (count % 16).astype(F32)
    meta = two_rows((EXT, CH), high, low)
    for z in range(NZ):
        kv_ref[z, 0:TB, :] = turned
        kv_ref[z, TB : TB + EXT, :] = meta


def project_kernel(w_ref, grad_ref, queries_ref, spot_ref, _, x_ref):
    d_attn = dot(w_ref[...], grad_ref[...]).astype(BF)
    spot = spot_ref[0:1, :]
    place = place_matrix(spot)
    queries = queries_ref[...] * jnp.asarray(0.125, BF)
    x = dot_nt(jnp.concatenate([queries, d_attn], 0), place).astype(BF)
    n = jnp.max(spot, axis=1, keepdims=True) + 1.0
    high = jnp.floor(n / 16.0)
    meta = two_rows((EXT, TB), high, n - 16.0 * high)
    for y in range(NY):
        x_ref[y, 0 : 2 * HD, :] = x
        x_ref[y, 2 * HD : 2 * HD + EXT, :] = meta


def pack_keys(kv_ref, kvp_ref, sc_ref):
    lane = iota((TB, CH), 1)
    row = iota((TB, CH), 0)
    ones = jnp.where((lane >= 1) & (lane <= 3), 1.0, 0.0)
    offset = jnp.int32(0)
    for b in range(NZ):
        count = count_of(kv_ref[b, TB : TB + EXT, :])
        here = pl.multiple_of(offset, 16)
        kvp_ref[pl.ds(here, TB), 0:CH] = kv_ref[b, 0:TB, :]
        aux = jnp.where((lane == 0) & (row >= count), BIAS, ones)
        kvp_ref[pl.ds(here, TB), CH : 2 * CH] = aux.astype(BF)
        size = ((count + 15) // 16) * 16
        sc_ref[KEY_AT + b] = offset
        sc_ref[KEY_SIZE + b] = size
        offset = offset + size
    here = pl.multiple_of(offset, 16)
    kvp_ref[pl.ds(here, TK), 0:CH] = jnp.zeros((TK, CH), BF)
    kvp_ref[pl.ds(here, TK), CH : 2 * CH] = jnp.where(lane == 0, BIAS, ones)[0:TK].astype(BF)
    n_tiles = (offset + TK - 1) // TK
    sc_ref[KEY_TILES] = n_tiles
    return n_tiles


def transpose_keys(kvp_ref, kvt_ref, n_key_tiles):
    unit = eye(CH)
    kvt_ref[CH : CH + EXT, :] = jnp.where(iota((EXT, KPAD), 0) == 0, 1.0, 0.0).astype(BF)

    def one(kt, _):
        at = pl.multiple_of(kt * TK, TK)
        kvt_ref[0:CH, pl.ds(at, TK)] = dot_nt(unit, kvp_ref[pl.ds(at, TK), 0:CH]).astype(BF)
        return 0

    lax.fori_loop(0, n_key_tiles, one, 0)


def lane_window(offset):
    start = (offset // CH) * CH
    return pl.multiple_of(start, CH), offset - start


def pack_queries(x_ref, xp_ref, sc_ref):
    xp_ref[...] = jnp.zeros(xp_ref.shape, F32)
    offset = jnp.int32(0)
    for b in range(NY):
        count = count_of(x_ref[b, 2 * HD : 2 * HD + EXT, :])
        start, shift = lane_window(offset)
        block = x_ref[b, 0 : 2 * HD, :].astype(F32)
        block = jnp.concatenate([block, jnp.zeros((2 * HD, CH), F32)], 1)
        xp_ref[:, pl.ds(start, WIDE)] += pltpu.roll(block, shift, 1)
        sc_ref[QUERY_AT + b] = offset
        sc_ref[QUERY_SIZE + b] = count
        offset = offset + count
    n_tiles = (offset + TQ - 1) // TQ
    sc_ref[QUERY_TILES] = n_tiles
    return n_tiles


def unpack_lanes(window, shift, count):
    back = pltpu.roll(window, (WIDE - shift) % WIDE, 1)[:, 0:TB]
    return jnp.where(iota(back.shape, 1) < count, back, 0.0)


def over_keys(n_key_tiles, step, state):
    big = n_key_tiles // 4
    state = lax.fori_loop(0, big, lambda i, s: step(i * 4 * TK, 4 * TK, s), state)
    half = (n_key_tiles // 2) % 2
    state = lax.fori_loop(0, half, lambda i, s: step(big * 4 * TK, 2 * TK, s), state)
    last = n_key_tiles % 2
    return lax.fori_loop(0, last, lambda i, s: step((n_key_tiles - 1) * TK, TK, s), state)


def forward_kernel(kv_ref, x_ref, out_ref, sc_ref, kvp_ref, kvt_ref, xp_ref, ws_ref, acc_ref, st_ref):
    n_key_tiles = pack_keys(kv_ref, kvp_ref, sc_ref)
    transpose_keys(kvp_ref, kvt_ref, n_key_tiles)
    n_query_tiles = pack_queries(x_ref, xp_ref, sc_ref)
    ws_ref[...] = jnp.zeros(ws_ref.shape, BF)
    ws_ref[0:HD, :] = xp_ref[0:HD, :].astype(BF)
    ws_ref[CH : CH + EXT, :] = jnp.where(iota((EXT, QPAD), 0) == 0, 1.0, 0.0).astype(BF)
    st_ref[...] = jnp.where(iota((8, QPAD), 0) == 1, 1.0, 0.0)
    acc_ref[...] = jnp.zeros(acc_ref.shape, F32)

    def query_tile(qt, _):
        q0 = pl.multiple_of(qt * TQ, TQ)
        ws = ws_ref[:, pl.ds(q0, TQ)]

        def key_tile(k0, size, carry):
            top, acc = carry
            k0 = pl.multiple_of(k0, TK)
            s = dot(kvp_ref[pl.ds(k0, size), :], ws)
            new = jnp.maximum(top, jnp.max(s, axis=0, keepdims=True))
            e = jnp.exp(s - new).astype(BF)
            acc = acc * jnp.exp(top - new) + dot(kvt_ref[HD : CH + EXT, pl.ds(k0, size)], e)
            return new, acc

        start = (jnp.full((1, TQ), -1e30, F32), jnp.zeros((HD + EXT, TQ), F32))
        top, acc = over_keys(n_key_tiles, key_tile, start)
        total = acc[HD : HD + 1]
        dsum = jnp.sum(acc[0:HD] * xp_ref[HD : 2 * HD, pl.ds(q0, TQ)], axis=0, keepdims=True)
        acc_ref[:, pl.ds(q0, TQ)] = acc[0:HD] / total
        st_ref[0:1, pl.ds(q0, TQ)] = top
        st_ref[1:2, pl.ds(q0, TQ)] = total
        st_ref[2:3, pl.ds(q0, TQ)] = dsum
        return 0

    lax.fori_loop(0, n_query_tiles, query_tile, 0)

    rows = [st_ref[i : i + 1, q * TB : (q + 1) * TB] for i in range(3) for q in range(NY)]
    split = pieces(jnp.concatenate(rows + [jnp.zeros((4, TB), F32)], 0))
    for b in range(NY):
        start, shift = lane_window(sc_ref[QUERY_AT + b])
        part = unpack_lanes(acc_ref[:, pl.ds(start, WIDE)], shift, sc_ref[QUERY_SIZE + b])
        out_ref[b, 0:HD, :] = part.astype(BF)
        for i in range(3):
            out_ref[b, HD + i * EXT : HD + (i + 1) * EXT, :] = split[i]


def merged_stats(r_ref):
    stats = []
    for s in range(NY):
        st = r_ref[s, HD : HD + EXT, :].astype(F32)
        st = st + r_ref[s, HD + EXT : HD + 2 * EXT, :].astype(F32)
        stats.append(st + r_ref[s, HD + 2 * EXT : HD + 3 * EXT, :].astype(F32))
    top = stats[0][0:NY]
    for s in range(1, NY):
        top = jnp.maximum(top, stats[s][0:NY])
    shares = []
    total = jnp.zeros((NY, TB), F32)
    dsum = jnp.zeros((NY, TB), F32)
    for s in range(NY):
        fade = jnp.exp(stats[s][0:NY] - top)
        shares.append(stats[s][NY : 2 * NY] * fade)
        total = total + shares[s]
        dsum = dsum + stats[s][2 * NY : 3 * NY] * fade
    return top + jnp.log(total), dsum / total, [share / total for share in shares]


def combine_kernel(y_ref, sc_ref, r_ref, grad_ref, spot_ref, out_ref, share_ref):
    _, _, shares = merged_stats(r_ref)
    share_ref[...] = jnp.zeros(share_ref.shape, F32)
    for s in range(NY):
        for q in range(NY):
            share_ref[s : s + 1, q * TB : (q + 1) * TB] = shares[s][q : q + 1]
    own = y_ref[0]
    start, shift = lane_window(sc_ref[QUERY_AT + own])
    share = unpack_lanes(share_ref[:, pl.ds(start, WIDE)], shift, sc_ref[QUERY_SIZE + own])
    attn = jnp.zeros((HD, TB), F32)
    for s in range(NY):
        attn = attn + r_ref[s, 0:HD, :].astype(F32) * share[s : s + 1]
    attn = dot(attn.astype(BF), place_matrix(spot_ref[0:1, :])).astype(BF)
    for z in range(NZ):
        part = dot_nt(attn, grad_ref[z * CH : (z + 1) * CH, :])
        for y in range(NY):
            out_ref[y * NZ + z] = part[y * 16 : (y + 1) * 16, :].astype(BF)


def backward_kernel(
    kv_ref, x_ref, r_ref, dq_ref, dkv_ref, sc_ref, kvp_ref, kvt_ref, xp_ref, ws_ref, wd_ref, xq_ref, xd_ref, dqa_ref, dkva_ref
):
    n_key_tiles = pack_keys(kv_ref, kvp_ref, sc_ref)
    transpose_keys(kvp_ref, kvt_ref, n_key_tiles)
    n_query_tiles = pack_queries(x_ref, xp_ref, sc_ref)
    ws_ref[...] = jnp.zeros(ws_ref.shape, BF)
    wd_ref[...] = jnp.zeros(wd_ref.shape, BF)
    ws_ref[0:HD, :] = xp_ref[0:HD, :].astype(BF)
    wd_ref[HD : 2 * HD, :] = xp_ref[HD : 2 * HD, :].astype(BF)
    lse, delta, _ = merged_stats(r_ref)
    row = iota((EXT, TB), 0)
    lse_pieces = [piece.astype(F32) for piece in pieces(-lse)]
    delta_pieces = [piece.astype(F32) for piece in pieces(-delta)]
    for q in range(NY):
        tile_s = jnp.where(row == 0, 1.0, 0.0)
        tile_d = jnp.zeros((EXT, TB), F32)
        for i in range(3):
            tile_s = jnp.where(row == i + 1, lse_pieces[i][q : q + 1], tile_s)
            tile_d = jnp.where(row == i + 1, delta_pieces[i][q : q + 1], tile_d)
        ws_ref[CH : CH + EXT, q * TB : (q + 1) * TB] = tile_s.astype(BF)
        wd_ref[CH : CH + EXT, q * TB : (q + 1) * TB] = tile_d.astype(BF)

    unit = eye(TQ)

    def turn(qt, _):
        q0 = pl.multiple_of(qt * TQ, TQ)
        xq_ref[pl.ds(q0, TQ), :] = dot_nt(unit, ws_ref[0:CH, pl.ds(q0, TQ)]).astype(BF)
        xd_ref[pl.ds(q0, TQ), :] = dot_nt(unit, wd_ref[0:CH, pl.ds(q0, TQ)]).astype(BF)
        return 0

    lax.fori_loop(0, n_query_tiles, turn, 0)
    dqa_ref[...] = jnp.zeros(dqa_ref.shape, F32)

    def key_tile(k0, size, _):
        k0 = pl.multiple_of(k0, TK)
        kv = kvp_ref[pl.ds(k0, size), :]
        dkva_ref[pl.ds(k0, size), :] = jnp.zeros((size, CH), F32)

        def query_tile(qt, _):
            q0 = pl.multiple_of(qt * TQ, TQ)
            prob = jnp.exp(dot(kv, ws_ref[:, pl.ds(q0, TQ)]))
            dscore = (prob * dot(kv, wd_ref[:, pl.ds(q0, TQ)])).astype(BF)
            prob = prob.astype(BF)
            dqa_ref[:, pl.ds(q0, TQ)] += dot(kvt_ref[0:HD, pl.ds(k0, size)], dscore)
            acc = dot(dscore, xq_ref[pl.ds(q0, TQ), :]) + dot(prob, xd_ref[pl.ds(q0, TQ), :])
            dkva_ref[pl.ds(k0, size), :] += acc
            return 0

        lax.fori_loop(0, n_query_tiles, query_tile, 0)
        return 0

    over_keys(n_key_tiles, key_tile, 0)

    for b in range(NY):
        start, shift = lane_window(sc_ref[QUERY_AT + b])
        part = unpack_lanes(dqa_ref[:, pl.ds(start, WIDE)], shift, sc_ref[QUERY_SIZE + b])
        part = (0.125 * part).astype(BF)
        for c in range(NCH):
            dq_ref[b, c * HD : (c + 1) * HD, :] = part[:, c * CH : (c + 1) * CH]
    krow = iota((TB, CH), 0)
    for b in range(NZ):
        got = dkva_ref[pl.ds(pl.multiple_of(sc_ref[KEY_AT + b], 16), TB), :]
        dkv_ref[b, 0:TB, :] = jnp.where(krow < sc_ref[KEY_SIZE + b], got, 0.0).astype(BF)
        dkv_ref[b, TB : TB + EXT, :] = jnp.zeros((EXT, CH), BF)


def keys_out_kernel(got_ref, dk_ref, dv_ref):
    total = got_ref[0, 0:TB, :].astype(F32)
    for z in range(1, NZ):
        total = total + got_ref[z, 0:TB, :].astype(F32)
    turned = dot_nt(eye(CH), total.astype(BF)).astype(BF)
    dk_ref[...] = turned[0:HD]
    dv_ref[...] = turned[HD:]


def rest_out_kernel(got_ref, spot_ref, dq_ref, dw_ref):
    place = place_matrix(spot_ref[0:1, :])
    total = got_ref[0, 0 : NCH * HD, :].astype(F32)
    for y in range(1, NY):
        total = total + got_ref[y, 0 : NCH * HD, :].astype(F32)
    total = total.astype(BF)
    dq = dot(total[0:HD], place[0:CH])
    for c in range(1, NCH):
        dq = dq + dot(total[c * HD : (c + 1) * HD], place[c * CH : (c + 1) * CH])
    dq_ref[...] = dq.astype(BF)
    base = NCH * HD
    for y in range(NY):
        for z in range(NZ):
            part = got_ref[y, base + z * 16 : base + (z + 1) * 16, :]
            dw_ref[y * 16 : (y + 1) * 16, z * CH : (z + 1) * CH] = part.astype(F32)


VMEM = pl.BlockSpec(memory_space=pltpu.VMEM)
BLOCK = pl.BlockSpec()
SMEM = pl.BlockSpec(memory_space=pltpu.SMEM)
ANY = pl.BlockSpec(memory_space=pl.ANY)
MIB = 1024 * 1024


def call(kernel, name, outs, ins, out_spaces, scratch, flops, args, limit=8):
    return pl.pallas_call(
        kernel,
        out_shape=tuple(jax.ShapeDtypeStruct(s, d) for s, d in outs),
        in_specs=ins,
        out_specs=tuple(out_spaces),
        scratch_shapes=[pltpu.VMEM(s, d) for s, d in scratch],
        compiler_params=pltpu.CompilerParams(vmem_limit_bytes=limit * MIB),
        cost_estimate=pl.CostEstimate(flops=flops, bytes_accessed=10**6, transcendentals=0),
        name=name,
    )(*args)


def prepare(count, keys, values, out_grad, keep):
    outs = [((NZ, TB + EXT, CH), BF), ((HD, TB), BF), ((8, TB), F32)]
    args = (count, keys, values, out_grad, keep)
    return call(prepare_kernel, "prepare", outs, [SMEM] + [BLOCK] * 3 + [VMEM], [VMEM] * 3, [], 10**8, args)


def project(w_out, grad_all, queries, spot, after):
    outs = [((NY, 2 * HD + EXT, TB), BF)]
    args = (w_out, grad_all, queries, spot, after)
    return call(project_kernel, "project", outs, [BLOCK, VMEM, BLOCK, VMEM, ANY], [VMEM], [], 10**8, args)[0]


PACKED = [((KPAD, 2 * CH), BF), ((CH + EXT, KPAD), BF), ((2 * HD, QPAD), F32), ((2 * CH, QPAD), BF)]


def forward(kv_all, x_all):
    outs = [((NY, HD + 3 * EXT, TB), BF), ((32,), jnp.int32)]
    scratch = PACKED + [((HD, QPAD), F32), ((8, QPAD), F32)]
    args = (kv_all, x_all)
    return call(forward_kernel, "forward", outs, [VMEM] * 2, [VMEM, SMEM], scratch, 4 * 10**9, args, 20)


def combine(own, sc, got, grad_all, spot):
    outs = [((NY * NZ, 16, CH), BF)]
    args = (own, sc, got, grad_all, spot)
    return call(combine_kernel, "combine", outs, [SMEM] * 2 + [VMEM] * 3, [VMEM], [((8, QPAD), F32)], 10**8, args)[0]


def backward(kv_all, x_all, got):
    outs = [((NY, NCH * HD, CH), BF), ((NZ, TB + EXT, CH), BF), ((32,), jnp.int32)]
    scratch = PACKED + [
        ((2 * CH, QPAD), BF),
        ((QPAD, CH), BF),
        ((QPAD, CH), BF),
        ((HD, QPAD), F32),
        ((KPAD, CH), F32),
    ]
    args = (kv_all, x_all, got)
    return call(backward_kernel, "backward", outs, [VMEM] * 3, [VMEM] * 2 + [SMEM], scratch, 8 * 10**9, args, 20)


def keys_out(got):
    outs = [((HD, TB), BF), ((HD, TB), BF)]
    return call(keys_out_kernel, "keys_out", outs, [VMEM], [VMEM] * 2, [], 10**7, (got,))


def rest_out(got, spot):
    outs = [((HD, TB), BF), ((HD, D), F32)]
    return call(rest_out_kernel, "rest_out", outs, [VMEM] * 2, [VMEM] * 2, [], 10**7, (got, spot))


def exchange(slots, axis, groups=None):
    return lax.all_to_all(slots, axis, 0, 0, tiled=True, axis_index_groups=groups)


def on_device(queries, keys, values, out_grad, w_out, counts, keep):
    kv, grad, spot = prepare(counts, keys, values, out_grad, keep.reshape(1, TB))
    kv_all = exchange(kv, "tok", Z_GROUPS)
    grad_all = lax.all_gather(grad, "head", axis=0, tiled=True)
    x_all = exchange(project(w_out, grad_all, queries, spot, kv_all), "tok", Y_GROUPS)
    slots, sc = forward(kv_all, x_all)
    got = exchange(slots, "tok", Y_GROUPS)
    own = (lax.axis_index("tok") // NZ).astype(jnp.int32).reshape(1)
    parts = exchange(combine(own, sc, got, grad_all, spot), "tok")
    dq_parts, dkv_parts, _ = backward(kv_all, x_all, got)
    piece = jnp.sum(parts.astype(F32), axis=0).astype(BF)
    dkv_parts = dkv_parts.at[:, TB:, :].set(piece[None])
    dkv_got = exchange(dkv_parts, "tok", Z_GROUPS)
    row_pieces = dkv_got[:, TB:, :].reshape(1, NZ * 16, CH)
    last = jnp.concatenate([dq_parts, jnp.broadcast_to(row_pieces, (NY, NZ * 16, CH))], 1)
    last = exchange(last, "tok", Y_GROUPS)
    dk, dv = keys_out(dkv_got)
    dq, d_wout = rest_out(last, spot)
    return dq, dk, dv, d_wout


def solution(mesh):
    return jax.shard_map(
        on_device,
        mesh=mesh,
        in_specs=(
            P("head", "tok"),
            P("head", "tok"),
            P("head", "tok"),
            P("head", "tok"),
            P("head", None),
            P("tok"),
            P("tok"),
        ),
        out_specs=(P("head", "tok"), P("head", "tok"), P("head", "tok"), P("head", None)),
        check_vma=False,
    )
```

```python
import jax
import jax.numpy as jnp
from jax import lax
from jax.experimental import pallas as pl
from jax.experimental.pallas import tpu as pltpu
from jax.sharding import PartitionSpec as P

HD = 64
D = 1024
TB = 384
NY = 4
NZ = 8
CH = 128
NCH = TB // CH
TK = 256
TQ = 256
KROWS = NZ * TB
QCOLS = NY * TB
KPAD = KROWS + TB
QPAD = QCOLS + CH
WIDE = TB + CH
EXT = 16
BIAS = -30000.0
BF = jnp.bfloat16
F32 = jnp.float32
Z_GROUPS = [[y * NZ + z for z in range(NZ)] for y in range(NY)]
Y_GROUPS = [[y * NZ + z for y in range(NY)] for z in range(NZ)]
KEY_AT, KEY_SIZE, QUERY_AT, QUERY_SIZE, KEY_TILES, QUERY_TILES = 0, 8, 16, 20, 24, 25


def dot(a, b):
    return jnp.dot(a, b, preferred_element_type=F32)


def dot_nt(a, b):
    return lax.dot_general(a, b, (((1,), (1,)), ((), ())), preferred_element_type=F32)


def iota(shape, dim):
    return lax.broadcasted_iota(jnp.int32, shape, dim)


def eye(n):
    return jnp.where(iota((n, n), 0) == iota((n, n), 1), 1.0, 0.0).astype(BF)


def pieces(x):
    hi = x.astype(BF)
    rest = x - hi.astype(F32)
    mid = rest.astype(BF)
    low = (rest - mid.astype(F32)).astype(BF)
    return hi, mid, low


def two_rows(shape, first, second):
    row = iota(shape, 0)
    return jnp.where(row == 0, first, jnp.where(row == 1, second, 0.0)).astype(BF)


def count_of(meta):
    meta = meta.astype(F32)
    return jnp.max(meta[0:1, 0:CH] * 16.0 + meta[1:2, 0:CH]).astype(jnp.int32)


def place_matrix(spot):
    return jnp.where(iota((TB, TB), 0).astype(F32) == spot, 1.0, 0.0).astype(BF)


def prepare_kernel(
    count_ref, keys_ref, values_ref, out_grad_ref, keep_ref, kv_ref, grad_ref, spot_ref, both_ref, held_ref, kept_ref, sems
):
    loads = [
        pltpu.make_async_copy(keep_ref, kept_ref, sems.at[0]),
        pltpu.make_async_copy(out_grad_ref, held_ref, sems.at[1]),
        pltpu.make_async_copy(keys_ref, both_ref.at[0:HD], sems.at[2]),
        pltpu.make_async_copy(values_ref, both_ref.at[HD : 2 * HD], sems.at[3]),
    ]
    for load in loads:
        load.start()
    count = count_ref[0]
    upto = jnp.where(iota((TB, TB), 0) <= iota((TB, TB), 1), 1.0, 0.0).astype(BF)
    loads[0].wait()
    keep = jnp.broadcast_to(kept_ref[...].astype(F32)[None, :], (8, TB))
    live = jnp.where(iota((8, TB), 1) < count, keep, 0.0)
    order = dot(live.astype(BF), upto)
    spot_ref[...] = jnp.where(live > 0.0, order - 1.0, -1.0)
    loads[1].wait()
    grad_ref[...] = held_ref[...] * live[0:1].astype(BF)
    loads[2].wait()
    loads[3].wait()
    turned = dot_nt(eye(TB), both_ref[...]).astype(BF)
    high = (count // 16).astype(F32)
    low = (count % 16).astype(F32)
    meta = two_rows((EXT, CH), high, low)
    for z in range(NZ):
        kv_ref[z, 0:TB, :] = turned
        kv_ref[z, TB : TB + EXT, :] = meta


def project_kernel(w_ref, grad_ref, queries_ref, spot_ref, _, x_ref):
    d_attn = dot(w_ref[...], grad_ref[...]).astype(BF)
    spot = spot_ref[0:1, :]
    place = place_matrix(spot)
    queries = queries_ref[...] * jnp.asarray(0.125, BF)
    x = dot_nt(jnp.concatenate([queries, d_attn], 0), place).astype(BF)
    n = jnp.max(spot, axis=1, keepdims=True) + 1.0
    high = jnp.floor(n / 16.0)
    meta = two_rows((EXT, TB), high, n - 16.0 * high)
    for y in range(NY):
        x_ref[y, 0 : 2 * HD, :] = x
        x_ref[y, 2 * HD : 2 * HD + EXT, :] = meta


def pack_keys(kv_ref, kvp_ref, sc_ref):
    lane = iota((TB, CH), 1)
    row = iota((TB, CH), 0)
    ones = jnp.where((lane >= 1) & (lane <= 3), 1.0, 0.0)
    offset = jnp.int32(0)
    for b in range(NZ):
        count = count_of(kv_ref[b, TB : TB + EXT, :])
        here = pl.multiple_of(offset, 16)
        kvp_ref[pl.ds(here, TB), 0:CH] = kv_ref[b, 0:TB, :]
        aux = jnp.where((lane == 0) & (row >= count), BIAS, ones)
        kvp_ref[pl.ds(here, TB), CH : 2 * CH] = aux.astype(BF)
        size = ((count + 15) // 16) * 16
        sc_ref[KEY_AT + b] = offset
        sc_ref[KEY_SIZE + b] = size
        offset = offset + size
    here = pl.multiple_of(offset, 16)
    kvp_ref[pl.ds(here, TK), 0:CH] = jnp.zeros((TK, CH), BF)
    kvp_ref[pl.ds(here, TK), CH : 2 * CH] = jnp.where(lane == 0, BIAS, ones)[0:TK].astype(BF)
    n_tiles = (offset + TK - 1) // TK
    sc_ref[KEY_TILES] = n_tiles
    return n_tiles


def transpose_keys(kvp_ref, kvt_ref, n_key_tiles):
    unit = eye(CH)
    kvt_ref[CH : CH + EXT, :] = jnp.where(iota((EXT, KPAD), 0) == 0, 1.0, 0.0).astype(BF)

    def one(kt, _):
        at = pl.multiple_of(kt * TK, TK)
        kvt_ref[0:CH, pl.ds(at, TK)] = dot_nt(unit, kvp_ref[pl.ds(at, TK), 0:CH]).astype(BF)
        return 0

    lax.fori_loop(0, n_key_tiles, one, 0)


def lane_window(offset):
    start = (offset // CH) * CH
    return pl.multiple_of(start, CH), offset - start


def pack_queries(x_ref, xp_ref, sc_ref):
    xp_ref[...] = jnp.zeros(xp_ref.shape, F32)
    offset = jnp.int32(0)
    for b in range(NY):
        count = count_of(x_ref[b, 2 * HD : 2 * HD + EXT, :])
        start, shift = lane_window(offset)
        block = x_ref[b, 0 : 2 * HD, :].astype(F32)
        block = jnp.concatenate([block, jnp.zeros((2 * HD, CH), F32)], 1)
        xp_ref[:, pl.ds(start, WIDE)] += pltpu.roll(block, shift, 1)
        sc_ref[QUERY_AT + b] = offset
        sc_ref[QUERY_SIZE + b] = count
        offset = offset + count
    n_tiles = (offset + TQ - 1) // TQ
    sc_ref[QUERY_TILES] = n_tiles
    return n_tiles


def unpack_lanes(window, shift, count):
    back = pltpu.roll(window, (WIDE - shift) % WIDE, 1)[:, 0:TB]
    return jnp.where(iota(back.shape, 1) < count, back, 0.0)


def over_keys(n_key_tiles, step, state):
    big = n_key_tiles // 4
    state = lax.fori_loop(0, big, lambda i, s: step(i * 4 * TK, 4 * TK, s), state)
    half = (n_key_tiles // 2) % 2
    state = lax.fori_loop(0, half, lambda i, s: step(big * 4 * TK, 2 * TK, s), state)
    last = n_key_tiles % 2
    return lax.fori_loop(0, last, lambda i, s: step((n_key_tiles - 1) * TK, TK, s), state)


def forward_kernel(kv_ref, x_ref, out_ref, sc_ref, kvp_ref, kvt_ref, xp_ref, ws_ref, acc_ref, st_ref):
    n_key_tiles = pack_keys(kv_ref, kvp_ref, sc_ref)
    transpose_keys(kvp_ref, kvt_ref, n_key_tiles)
    n_query_tiles = pack_queries(x_ref, xp_ref, sc_ref)
    ws_ref[...] = jnp.zeros(ws_ref.shape, BF)
    ws_ref[0:HD, :] = xp_ref[0:HD, :].astype(BF)
    ws_ref[CH : CH + EXT, :] = jnp.where(iota((EXT, QPAD), 0) == 0, 1.0, 0.0).astype(BF)
    st_ref[...] = jnp.where(iota((8, QPAD), 0) == 1, 1.0, 0.0)
    acc_ref[...] = jnp.zeros(acc_ref.shape, F32)

    def query_tile(qt, _):
        q0 = pl.multiple_of(qt * TQ, TQ)
        ws = ws_ref[:, pl.ds(q0, TQ)]

        def key_tile(k0, size, carry):
            top, acc = carry
            k0 = pl.multiple_of(k0, TK)
            s = dot(kvp_ref[pl.ds(k0, size), :], ws)
            new = jnp.maximum(top, jnp.max(s, axis=0, keepdims=True))
            e = jnp.exp(s - new).astype(BF)
            acc = acc * jnp.exp(top - new) + dot(kvt_ref[HD : CH + EXT, pl.ds(k0, size)], e)
            return new, acc

        start = (jnp.full((1, TQ), -1e30, F32), jnp.zeros((HD + EXT, TQ), F32))
        top, acc = over_keys(n_key_tiles, key_tile, start)
        total = acc[HD : HD + 1]
        dsum = jnp.sum(acc[0:HD] * xp_ref[HD : 2 * HD, pl.ds(q0, TQ)], axis=0, keepdims=True)
        acc_ref[:, pl.ds(q0, TQ)] = acc[0:HD] / total
        st_ref[0:1, pl.ds(q0, TQ)] = top
        st_ref[1:2, pl.ds(q0, TQ)] = total
        st_ref[2:3, pl.ds(q0, TQ)] = dsum
        return 0

    lax.fori_loop(0, n_query_tiles, query_tile, 0)

    rows = [st_ref[i : i + 1, q * TB : (q + 1) * TB] for i in range(3) for q in range(NY)]
    split = pieces(jnp.concatenate(rows + [jnp.zeros((4, TB), F32)], 0))
    for b in range(NY):
        start, shift = lane_window(sc_ref[QUERY_AT + b])
        part = unpack_lanes(acc_ref[:, pl.ds(start, WIDE)], shift, sc_ref[QUERY_SIZE + b])
        out_ref[b, 0:HD, :] = part.astype(BF)
        for i in range(3):
            out_ref[b, HD + i * EXT : HD + (i + 1) * EXT, :] = split[i]


def merged_stats(r_ref):
    stats = []
    for s in range(NY):
        st = r_ref[s, HD : HD + EXT, :].astype(F32)
        st = st + r_ref[s, HD + EXT : HD + 2 * EXT, :].astype(F32)
        stats.append(st + r_ref[s, HD + 2 * EXT : HD + 3 * EXT, :].astype(F32))
    top = stats[0][0:NY]
    for s in range(1, NY):
        top = jnp.maximum(top, stats[s][0:NY])
    shares = []
    total = jnp.zeros((NY, TB), F32)
    dsum = jnp.zeros((NY, TB), F32)
    for s in range(NY):
        fade = jnp.exp(stats[s][0:NY] - top)
        shares.append(stats[s][NY : 2 * NY] * fade)
        total = total + shares[s]
        dsum = dsum + stats[s][2 * NY : 3 * NY] * fade
    return top + jnp.log(total), dsum / total, [share / total for share in shares]


def combine_kernel(y_ref, sc_ref, r_ref, grad_ref, spot_ref, out_ref, share_ref):
    _, _, shares = merged_stats(r_ref)
    share_ref[...] = jnp.zeros(share_ref.shape, F32)
    for s in range(NY):
        for q in range(NY):
            share_ref[s : s + 1, q * TB : (q + 1) * TB] = shares[s][q : q + 1]
    own = y_ref[0]
    start, shift = lane_window(sc_ref[QUERY_AT + own])
    share = unpack_lanes(share_ref[:, pl.ds(start, WIDE)], shift, sc_ref[QUERY_SIZE + own])
    attn = jnp.zeros((HD, TB), F32)
    for s in range(NY):
        attn = attn + r_ref[s, 0:HD, :].astype(F32) * share[s : s + 1]
    attn = dot(attn.astype(BF), place_matrix(spot_ref[0:1, :])).astype(BF)
    for z in range(NZ):
        part = dot_nt(attn, grad_ref[z * CH : (z + 1) * CH, :]).astype(BF)
        for y in range(NY):
            out_ref[y * NZ + z] = part


def backward_kernel(
    kv_ref, x_ref, r_ref, dq_ref, dkv_ref, sc_ref, kvp_ref, kvt_ref, xp_ref, ws_ref, wd_ref, xq_ref, xd_ref, dqa_ref, dkva_ref
):
    n_key_tiles = pack_keys(kv_ref, kvp_ref, sc_ref)
    transpose_keys(kvp_ref, kvt_ref, n_key_tiles)
    n_query_tiles = pack_queries(x_ref, xp_ref, sc_ref)
    ws_ref[...] = jnp.zeros(ws_ref.shape, BF)
    wd_ref[...] = jnp.zeros(wd_ref.shape, BF)
    ws_ref[0:HD, :] = xp_ref[0:HD, :].astype(BF)
    wd_ref[HD : 2 * HD, :] = xp_ref[HD : 2 * HD, :].astype(BF)
    lse, delta, _ = merged_stats(r_ref)
    row = iota((EXT, TB), 0)
    lse_pieces = [piece.astype(F32) for piece in pieces(-lse)]
    delta_pieces = [piece.astype(F32) for piece in pieces(-delta)]
    for q in range(NY):
        tile_s = jnp.where(row == 0, 1.0, 0.0)
        tile_d = jnp.zeros((EXT, TB), F32)
        for i in range(3):
            tile_s = jnp.where(row == i + 1, lse_pieces[i][q : q + 1], tile_s)
            tile_d = jnp.where(row == i + 1, delta_pieces[i][q : q + 1], tile_d)
        ws_ref[CH : CH + EXT, q * TB : (q + 1) * TB] = tile_s.astype(BF)
        wd_ref[CH : CH + EXT, q * TB : (q + 1) * TB] = tile_d.astype(BF)

    unit = eye(TQ)

    def turn(qt, _):
        q0 = pl.multiple_of(qt * TQ, TQ)
        xq_ref[pl.ds(q0, TQ), :] = dot_nt(unit, ws_ref[0:CH, pl.ds(q0, TQ)]).astype(BF)
        xd_ref[pl.ds(q0, TQ), :] = dot_nt(unit, wd_ref[0:CH, pl.ds(q0, TQ)]).astype(BF)
        return 0

    lax.fori_loop(0, n_query_tiles, turn, 0)
    dqa_ref[...] = jnp.zeros(dqa_ref.shape, F32)

    def key_tile(k0, size, _):
        k0 = pl.multiple_of(k0, TK)
        kv = kvp_ref[pl.ds(k0, size), :]
        dkva_ref[pl.ds(k0, size), :] = jnp.zeros((size, CH), F32)

        def query_tile(qt, _):
            q0 = pl.multiple_of(qt * TQ, TQ)
            prob = jnp.exp(dot(kv, ws_ref[:, pl.ds(q0, TQ)]))
            dscore = (prob * dot(kv, wd_ref[:, pl.ds(q0, TQ)])).astype(BF)
            prob = prob.astype(BF)
            dqa_ref[:, pl.ds(q0, TQ)] += dot(kvt_ref[0:HD, pl.ds(k0, size)], dscore)
            acc = dot(dscore, xq_ref[pl.ds(q0, TQ), :]) + dot(prob, xd_ref[pl.ds(q0, TQ), :])
            dkva_ref[pl.ds(k0, size), :] += acc
            return 0

        lax.fori_loop(0, n_query_tiles, query_tile, 0)
        return 0

    over_keys(n_key_tiles, key_tile, 0)

    for b in range(NY):
        start, shift = lane_window(sc_ref[QUERY_AT + b])
        part = unpack_lanes(dqa_ref[:, pl.ds(start, WIDE)], shift, sc_ref[QUERY_SIZE + b])
        for c in range(NCH):
            dq_ref[b, c * HD : (c + 1) * HD, :] = (0.125 * part[:, c * CH : (c + 1) * CH]).astype(BF)
    krow = iota((TB, CH), 0)
    for b in range(NZ):
        got = dkva_ref[pl.ds(pl.multiple_of(sc_ref[KEY_AT + b], 16), TB), :]
        dkv_ref[b, 0:TB, :] = jnp.where(krow < sc_ref[KEY_SIZE + b], got, 0.0).astype(BF)
        dkv_ref[b, TB : TB + HD, :] = jnp.zeros((HD, CH), BF)


def finish_kernel(y_ref, got_ref, dq_in_ref, spot_ref, dq_ref, dk_ref, dv_ref, dw_ref):
    total = got_ref[0, 0:TB, :].astype(F32)
    for z in range(1, NZ):
        total = total + got_ref[z, 0:TB, :].astype(F32)
    turned = dot_nt(eye(CH), total.astype(BF)).astype(BF)
    dk_ref[...] = turned[0:HD]
    dv_ref[...] = turned[HD:]
    for z in range(NZ):
        dw_ref[:, z * CH : (z + 1) * CH] = got_ref[z, TB : TB + HD, :].astype(F32)
    place = place_matrix(spot_ref[0:1, :])
    own = y_ref[0]
    dq_sum = dq_in_ref[0, own].astype(F32)
    for y in range(1, NY):
        dq_sum = dq_sum + dq_in_ref[y, own].astype(F32)
    dq_sum = dq_sum.astype(BF)
    dq = dot(dq_sum[0:HD], place[0:CH])
    for c in range(1, NCH):
        dq = dq + dot(dq_sum[c * HD : (c + 1) * HD], place[c * CH : (c + 1) * CH])
    dq_ref[...] = dq.astype(BF)


VMEM = pl.BlockSpec(memory_space=pltpu.VMEM)
BLOCK = pl.BlockSpec()
SMEM = pl.BlockSpec(memory_space=pltpu.SMEM)
ANY = pl.BlockSpec(memory_space=pl.ANY)
MIB = 1024 * 1024


def call(kernel, name, outs, ins, out_spaces, scratch, flops, args, limit=8):
    return pl.pallas_call(
        kernel,
        out_shape=tuple(jax.ShapeDtypeStruct(s, d) for s, d in outs),
        in_specs=ins,
        out_specs=tuple(out_spaces),
        scratch_shapes=[pltpu.VMEM(*item) if isinstance(item, tuple) else item for item in scratch],
        compiler_params=pltpu.CompilerParams(vmem_limit_bytes=limit * MIB),
        cost_estimate=pl.CostEstimate(flops=flops, bytes_accessed=10**6, transcendentals=0),
        name=name,
    )(*args)


def prepare(count, keys, values, out_grad, keep):
    outs = [((NZ, TB + EXT, CH), BF), ((HD, TB), BF), ((8, TB), F32)]
    scratch = [((2 * HD, TB), BF), ((HD, TB), BF), ((TB,), jnp.int32), pltpu.SemaphoreType.DMA((4,))]
    args = (count, keys, values, out_grad, keep)
    return call(prepare_kernel, "prepare", outs, [SMEM] + [ANY] * 4, [VMEM] * 3, scratch, 10**8, args, 56)


def project(w_out, grad_all, queries, spot, after):
    outs = [((NY, 2 * HD + EXT, TB), BF)]
    args = (w_out, grad_all, queries, spot, after)
    return call(project_kernel, "project", outs, [BLOCK, VMEM, BLOCK, VMEM, ANY], [VMEM], [], 10**8, args)[0]


PACKED = [((KPAD, 2 * CH), BF), ((CH + EXT, KPAD), BF), ((2 * HD, QPAD), F32), ((2 * CH, QPAD), BF)]


def forward(kv_all, x_all):
    outs = [((NY, HD + 3 * EXT, TB), BF), ((32,), jnp.int32)]
    scratch = PACKED + [((HD, QPAD), F32), ((8, QPAD), F32)]
    args = (kv_all, x_all)
    return call(forward_kernel, "forward", outs, [VMEM] * 2, [VMEM, SMEM], scratch, 4 * 10**9, args, 20)


def combine(own, sc, got, grad_all, spot):
    outs = [((NY * NZ, HD, CH), BF)]
    args = (own, sc, got, grad_all, spot)
    return call(combine_kernel, "combine", outs, [SMEM] * 2 + [VMEM] * 3, [VMEM], [((8, QPAD), F32)], 10**8, args)[0]


def backward(kv_all, x_all, got):
    outs = [((NY, NCH * HD, CH), BF), ((NZ, TB + HD, CH), BF), ((32,), jnp.int32)]
    scratch = PACKED + [
        ((2 * CH, QPAD), BF),
        ((QPAD, CH), BF),
        ((QPAD, CH), BF),
        ((HD, QPAD), F32),
        ((KPAD, CH), F32),
    ]
    args = (kv_all, x_all, got)
    return call(backward_kernel, "backward", outs, [VMEM] * 3, [VMEM] * 2 + [SMEM], scratch, 8 * 10**9, args, 20)


def finish(got, dq_all, spot, own):
    outs = [((HD, TB), BF), ((HD, TB), BF), ((HD, TB), BF), ((HD, D), F32)]
    args = (own, got, dq_all, spot)
    return call(finish_kernel, "finish", outs, [SMEM] + [VMEM] * 3, [VMEM] * 4, [], 10**7, args)


def exchange(slots, axis, groups=None):
    return lax.all_to_all(slots, axis, 0, 0, tiled=True, axis_index_groups=groups)


def on_device(queries, keys, values, out_grad, w_out, counts, keep):
    kv, grad, spot = prepare(counts, keys, values, out_grad, keep)
    kv_all = exchange(kv, "tok", Z_GROUPS)
    grad_all = lax.all_gather(grad, "head", axis=0, tiled=True)
    x_all = exchange(project(w_out, grad_all, queries, spot, kv_all), "tok", Y_GROUPS)
    slots, sc = forward(kv_all, x_all)
    got = exchange(slots, "tok", Y_GROUPS)
    own = (lax.axis_index("tok") // NZ).astype(jnp.int32).reshape(1)
    parts = exchange(combine(own, sc, got, grad_all, spot), "tok")
    dq_parts, dkv_parts, _ = backward(kv_all, x_all, got)
    dq_all = lax.all_gather(dq_parts, "tok", axis=0, axis_index_groups=Y_GROUPS)
    piece = jnp.sum(parts.astype(F32), axis=0).astype(BF)
    dkv_parts = dkv_parts.at[:, TB:, :].set(piece[None])
    return finish(exchange(dkv_parts, "tok", Z_GROUPS), dq_all, spot, own)


def solution(mesh):
    return jax.shard_map(
        on_device,
        mesh=mesh,
        in_specs=(
            P("head", "tok"),
            P("head", "tok"),
            P("head", "tok"),
            P("head", "tok"),
            P("head", None),
            P("tok"),
            P("tok"),
        ),
        out_specs=(P("head", "tok"), P("head", "tok"), P("head", "tok"), P("head", None)),
        check_vma=False,
    )
```

```python
import jax
import jax.numpy as jnp
from jax import lax
from jax.experimental import pallas as pl
from jax.experimental.pallas import tpu as pltpu
from jax.sharding import PartitionSpec as P

HD = 64
D = 1024
TB = 384
NY = 4
NZ = 8
CH = 128
NCH = TB // CH
TK = 256
TQ = 256
KROWS = NZ * TB
QCOLS = NY * TB
KPAD = KROWS + TB
QPAD = QCOLS + CH
WIDE = TB + CH
EXT = 16
BIAS = -30000.0
BF = jnp.bfloat16
F32 = jnp.float32
Z_GROUPS = [[y * NZ + z for z in range(NZ)] for y in range(NY)]
Y_GROUPS = [[y * NZ + z for y in range(NY)] for z in range(NZ)]
KEY_AT, KEY_SIZE, QUERY_AT, QUERY_SIZE, KEY_TILES, QUERY_TILES = 0, 8, 16, 20, 24, 25


def dot(a, b):
    return jnp.dot(a, b, preferred_element_type=F32)


def dot_nt(a, b):
    return lax.dot_general(a, b, (((1,), (1,)), ((), ())), preferred_element_type=F32)


def iota(shape, dim):
    return lax.broadcasted_iota(jnp.int32, shape, dim)


def eye(n):
    return jnp.where(iota((n, n), 0) == iota((n, n), 1), 1.0, 0.0).astype(BF)


def pieces(x):
    hi = x.astype(BF)
    rest = x - hi.astype(F32)
    mid = rest.astype(BF)
    low = (rest - mid.astype(F32)).astype(BF)
    return hi, mid, low


def two_rows(shape, first, second):
    row = iota(shape, 0)
    return jnp.where(row == 0, first, jnp.where(row == 1, second, 0.0)).astype(BF)


def count_of(meta):
    meta = meta.astype(F32)
    return jnp.max(meta[0:1, 0:CH] * 16.0 + meta[1:2, 0:CH]).astype(jnp.int32)


def place_matrix(spot):
    return jnp.where(iota((TB, TB), 0).astype(F32) == spot, 1.0, 0.0).astype(BF)


def prepare_kernel(
    count_ref, keys_ref, values_ref, out_grad_ref, keep_ref, kv_ref, grad_ref, spot_ref, both_ref, held_ref, kept_ref, sems
):
    loads = [
        pltpu.make_async_copy(keep_ref, kept_ref, sems.at[0]),
        pltpu.make_async_copy(out_grad_ref, held_ref, sems.at[1]),
        pltpu.make_async_copy(keys_ref, both_ref.at[0:HD], sems.at[2]),
        pltpu.make_async_copy(values_ref, both_ref.at[HD : 2 * HD], sems.at[3]),
    ]
    for load in loads:
        load.start()
    count = count_ref[0]
    upto = jnp.where(iota((TB, TB), 0) <= iota((TB, TB), 1), 1.0, 0.0).astype(BF)
    loads[0].wait()
    keep = jnp.broadcast_to(kept_ref[...].astype(F32)[None, :], (8, TB))
    live = jnp.where(iota((8, TB), 1) < count, keep, 0.0)
    order = dot(live.astype(BF), upto)
    spot_ref[...] = jnp.where(live > 0.0, order - 1.0, -1.0)
    loads[1].wait()
    grad_ref[...] = held_ref[...] * live[0:1].astype(BF)
    loads[2].wait()
    loads[3].wait()
    turned = dot_nt(eye(TB), both_ref[...]).astype(BF)
    high = (count // 16).astype(F32)
    low = (count % 16).astype(F32)
    meta = two_rows((EXT, CH), high, low)
    for z in range(NZ):
        kv_ref[z, 0:TB, :] = turned
        kv_ref[z, TB : TB + EXT, :] = meta


def project_kernel(w_ref, grad_ref, queries_ref, spot_ref, _, x_ref):
    d_attn = dot(w_ref[...], grad_ref[...]).astype(BF)
    spot = spot_ref[0:1, :]
    place = place_matrix(spot)
    queries = queries_ref[...] * jnp.asarray(0.125, BF)
    x = dot_nt(jnp.concatenate([queries, d_attn], 0), place).astype(BF)
    n = jnp.max(spot, axis=1, keepdims=True) + 1.0
    high = jnp.floor(n / 16.0)
    meta = two_rows((EXT, TB), high, n - 16.0 * high)
    for y in range(NY):
        x_ref[y, 0 : 2 * HD, :] = x
        x_ref[y, 2 * HD : 2 * HD + EXT, :] = meta


def pack_keys(kv_ref, kvp_ref, sc_ref):
    lane = iota((TB, CH), 1)
    row = iota((TB, CH), 0)
    ones = jnp.where((lane >= 1) & (lane <= 3), 1.0, 0.0)
    offset = jnp.int32(0)
    for b in range(NZ):
        count = count_of(kv_ref[b, TB : TB + EXT, :])
        here = pl.multiple_of(offset, 16)
        kvp_ref[pl.ds(here, TB), 0:CH] = kv_ref[b, 0:TB, :]
        aux = jnp.where((lane == 0) & (row >= count), BIAS, ones)
        kvp_ref[pl.ds(here, TB), CH : 2 * CH] = aux.astype(BF)
        size = ((count + 15) // 16) * 16
        sc_ref[KEY_AT + b] = offset
        sc_ref[KEY_SIZE + b] = size
        offset = offset + size
    here = pl.multiple_of(offset, 16)
    kvp_ref[pl.ds(here, TK), 0:CH] = jnp.zeros((TK, CH), BF)
    kvp_ref[pl.ds(here, TK), CH : 2 * CH] = jnp.where(lane == 0, BIAS, ones)[0:TK].astype(BF)
    n_tiles = (offset + TK - 1) // TK
    sc_ref[KEY_TILES] = n_tiles
    return n_tiles


def transpose_keys(kvp_ref, kvt_ref, n_key_tiles):
    unit = eye(CH)
    kvt_ref[CH : CH + EXT, :] = jnp.where(iota((EXT, KPAD), 0) == 0, 1.0, 0.0).astype(BF)

    def one(kt, _):
        at = pl.multiple_of(kt * TK, TK)
        kvt_ref[0:CH, pl.ds(at, TK)] = dot_nt(unit, kvp_ref[pl.ds(at, TK), 0:CH]).astype(BF)
        return 0

    lax.fori_loop(0, n_key_tiles, one, 0)


def lane_window(offset):
    start = (offset // CH) * CH
    return pl.multiple_of(start, CH), offset - start


def pack_queries(x_ref, xp_ref, sc_ref):
    xp_ref[...] = jnp.zeros(xp_ref.shape, F32)
    offset = jnp.int32(0)
    for b in range(NY):
        count = count_of(x_ref[b, 2 * HD : 2 * HD + EXT, :])
        start, shift = lane_window(offset)
        block = x_ref[b, 0 : 2 * HD, :].astype(F32)
        block = jnp.concatenate([block, jnp.zeros((2 * HD, CH), F32)], 1)
        xp_ref[:, pl.ds(start, WIDE)] += pltpu.roll(block, shift, 1)
        sc_ref[QUERY_AT + b] = offset
        sc_ref[QUERY_SIZE + b] = count
        offset = offset + count
    n_tiles = (offset + TQ - 1) // TQ
    sc_ref[QUERY_TILES] = n_tiles
    return n_tiles


def unpack_lanes(window, shift, count):
    back = pltpu.roll(window, (WIDE - shift) % WIDE, 1)[:, 0:TB]
    return jnp.where(iota(back.shape, 1) < count, back, 0.0)


def over_keys(n_key_tiles, step, state):
    big = n_key_tiles // 4
    state = lax.fori_loop(0, big, lambda i, s: step(i * 4 * TK, 4 * TK, s), state)
    half = (n_key_tiles // 2) % 2
    state = lax.fori_loop(0, half, lambda i, s: step(big * 4 * TK, 2 * TK, s), state)
    last = n_key_tiles % 2
    return lax.fori_loop(0, last, lambda i, s: step((n_key_tiles - 1) * TK, TK, s), state)


def forward_kernel(kv_ref, x_ref, out_ref, sc_ref, kvp_ref, kvt_ref, xp_ref, ws_ref, acc_ref, st_ref):
    n_key_tiles = pack_keys(kv_ref, kvp_ref, sc_ref)
    transpose_keys(kvp_ref, kvt_ref, n_key_tiles)
    n_query_tiles = pack_queries(x_ref, xp_ref, sc_ref)
    ws_ref[...] = jnp.zeros(ws_ref.shape, BF)
    ws_ref[0:HD, :] = xp_ref[0:HD, :].astype(BF)
    ws_ref[CH : CH + EXT, :] = jnp.where(iota((EXT, QPAD), 0) == 0, 1.0, 0.0).astype(BF)
    st_ref[...] = jnp.zeros(st_ref.shape, F32)
    acc_ref[...] = jnp.zeros(acc_ref.shape, F32)

    def query_tile(qt, _):
        q0 = pl.multiple_of(qt * TQ, TQ)
        ws = ws_ref[:, pl.ds(q0, TQ)]

        def key_tile(k0, size, carry):
            top, acc = carry
            k0 = pl.multiple_of(k0, TK)
            s = dot(kvp_ref[pl.ds(k0, size), :], ws)
            new = jnp.maximum(top, jnp.max(s, axis=0, keepdims=True))
            e = jnp.exp(s - new).astype(BF)
            acc = acc * jnp.exp(top - new) + dot(kvt_ref[HD : CH + EXT, pl.ds(k0, size)], e)
            return new, acc

        start = (jnp.full((1, TQ), -1e30, F32), jnp.zeros((HD + EXT, TQ), F32))
        top, acc = over_keys(n_key_tiles, key_tile, start)
        total = acc[HD : HD + 1]
        dsum = jnp.sum(acc[0:HD] * xp_ref[HD : 2 * HD, pl.ds(q0, TQ)], axis=0, keepdims=True)
        acc_ref[:, pl.ds(q0, TQ)] = acc[0:HD] / total
        st_ref[0:1, pl.ds(q0, TQ)] = top + jnp.log(total)
        st_ref[1:2, pl.ds(q0, TQ)] = dsum / total
        return 0

    lax.fori_loop(0, n_query_tiles, query_tile, 0)

    rows = [st_ref[i : i + 1, q * TB : (q + 1) * TB] for i in range(2) for q in range(NY)]
    split = [piece.astype(F32) for piece in pieces(jnp.concatenate(rows, 0))]
    stats = jnp.concatenate(split + [jnp.zeros((8, TB), F32)], 0).astype(BF)
    for b in range(NY):
        start, shift = lane_window(sc_ref[QUERY_AT + b])
        part = unpack_lanes(acc_ref[:, pl.ds(start, WIDE)], shift, sc_ref[QUERY_SIZE + b])
        out_ref[b, 0:HD, :] = part.astype(BF)
        out_ref[b, HD : HD + 2 * EXT, :] = stats


def merged_stats(r_ref):
    lses = []
    deltas = []
    for s in range(NY):
        st = r_ref[s, HD : HD + 2 * EXT, :].astype(F32)
        st = st[0:8] + st[8:16] + st[16:24]
        lses.append(st[0:NY])
        deltas.append(st[NY : 2 * NY])
    top = lses[0]
    for s in range(1, NY):
        top = jnp.maximum(top, lses[s])
    weights = [jnp.exp(lse - top) for lse in lses]
    total = weights[0] + weights[1] + weights[2] + weights[3]
    shares = [weight / total for weight in weights]
    delta = jnp.zeros((NY, TB), F32)
    for s in range(NY):
        delta = delta + shares[s] * deltas[s]
    return top + jnp.log(total), delta, shares


def combine_kernel(y_ref, sc_ref, r_ref, grad_ref, spot_ref, out_ref, share_ref):
    _, _, shares = merged_stats(r_ref)
    share_ref[...] = jnp.zeros(share_ref.shape, F32)
    for s in range(NY):
        for q in range(NY):
            share_ref[s : s + 1, q * TB : (q + 1) * TB] = shares[s][q : q + 1]
    own = y_ref[0]
    start, shift = lane_window(sc_ref[QUERY_AT + own])
    share = unpack_lanes(share_ref[:, pl.ds(start, WIDE)], shift, sc_ref[QUERY_SIZE + own])
    attn = jnp.zeros((HD, TB), F32)
    for s in range(NY):
        attn = attn + r_ref[s, 0:HD, :].astype(F32) * share[s : s + 1]
    attn = dot(attn.astype(BF), place_matrix(spot_ref[0:1, :])).astype(BF)
    for z in range(NZ):
        part = dot_nt(attn, grad_ref[z * CH : (z + 1) * CH, :]).astype(BF)
        for y in range(NY):
            out_ref[y * NZ + z] = part


def backward_kernel(
    kv_ref, x_ref, r_ref, dq_ref, dkv_ref, sc_ref, kvp_ref, kvt_ref, xp_ref, ws_ref, wd_ref, xq_ref, xd_ref, dqa_ref, dkva_ref
):
    n_key_tiles = pack_keys(kv_ref, kvp_ref, sc_ref)
    transpose_keys(kvp_ref, kvt_ref, n_key_tiles)
    n_query_tiles = pack_queries(x_ref, xp_ref, sc_ref)
    ws_ref[...] = jnp.zeros(ws_ref.shape, BF)
    wd_ref[...] = jnp.zeros(wd_ref.shape, BF)
    ws_ref[0:HD, :] = xp_ref[0:HD, :].astype(BF)
    wd_ref[HD : 2 * HD, :] = xp_ref[HD : 2 * HD, :].astype(BF)
    lse, delta, _ = merged_stats(r_ref)
    row = iota((EXT, TB), 0)
    lse_pieces = [piece.astype(F32) for piece in pieces(-lse)]
    delta_pieces = [piece.astype(F32) for piece in pieces(-delta)]
    for q in range(NY):
        tile_s = jnp.where(row == 0, 1.0, 0.0)
        tile_d = jnp.zeros((EXT, TB), F32)
        for i in range(3):
            tile_s = jnp.where(row == i + 1, lse_pieces[i][q : q + 1], tile_s)
            tile_d = jnp.where(row == i + 1, delta_pieces[i][q : q + 1], tile_d)
        ws_ref[CH : CH + EXT, q * TB : (q + 1) * TB] = tile_s.astype(BF)
        wd_ref[CH : CH + EXT, q * TB : (q + 1) * TB] = tile_d.astype(BF)

    unit = eye(TQ)

    def turn(qt, _):
        q0 = pl.multiple_of(qt * TQ, TQ)
        xq_ref[pl.ds(q0, TQ), :] = dot_nt(unit, ws_ref[0:CH, pl.ds(q0, TQ)]).astype(BF)
        xd_ref[pl.ds(q0, TQ), :] = dot_nt(unit, wd_ref[0:CH, pl.ds(q0, TQ)]).astype(BF)
        return 0

    lax.fori_loop(0, n_query_tiles, turn, 0)
    dqa_ref[...] = jnp.zeros(dqa_ref.shape, F32)

    def key_tile(k0, size, _):
        k0 = pl.multiple_of(k0, TK)
        kv = kvp_ref[pl.ds(k0, size), :]
        dkva_ref[pl.ds(k0, size), :] = jnp.zeros((size, CH), F32)

        def query_tile(qt, _):
            q0 = pl.multiple_of(qt * TQ, TQ)
            prob = jnp.exp(dot(kv, ws_ref[:, pl.ds(q0, TQ)]))
            dscore = (prob * dot(kv, wd_ref[:, pl.ds(q0, TQ)])).astype(BF)
            prob = prob.astype(BF)
            dqa_ref[:, pl.ds(q0, TQ)] += dot(kvt_ref[0:HD, pl.ds(k0, size)], dscore)
            acc = dot(dscore, xq_ref[pl.ds(q0, TQ), :]) + dot(prob, xd_ref[pl.ds(q0, TQ), :])
            dkva_ref[pl.ds(k0, size), :] += acc
            return 0

        lax.fori_loop(0, n_query_tiles, query_tile, 0)
        return 0

    over_keys(n_key_tiles, key_tile, 0)

    for b in range(NY):
        start, shift = lane_window(sc_ref[QUERY_AT + b])
        part = unpack_lanes(dqa_ref[:, pl.ds(start, WIDE)], shift, sc_ref[QUERY_SIZE + b])
        for c in range(NCH):
            dq_ref[b, c * HD : (c + 1) * HD, :] = (0.125 * part[:, c * CH : (c + 1) * CH]).astype(BF)
    krow = iota((TB, CH), 0)
    for b in range(NZ):
        got = dkva_ref[pl.ds(pl.multiple_of(sc_ref[KEY_AT + b], 16), TB), :]
        dkv_ref[b, 0:TB, :] = jnp.where(krow < sc_ref[KEY_SIZE + b], got, 0.0).astype(BF)
        dkv_ref[b, TB : TB + HD, :] = jnp.zeros((HD, CH), BF)


def finish_kernel(y_ref, got_ref, dq_in_ref, spot_ref, dq_ref, dk_ref, dv_ref, dw_ref):
    total = got_ref[0, 0:TB, :].astype(F32)
    for z in range(1, NZ):
        total = total + got_ref[z, 0:TB, :].astype(F32)
    turned = dot_nt(eye(CH), total.astype(BF)).astype(BF)
    dk_ref[...] = turned[0:HD]
    dv_ref[...] = turned[HD:]
    for z in range(NZ):
        dw_ref[:, z * CH : (z + 1) * CH] = got_ref[z, TB : TB + HD, :].astype(F32)
    place = place_matrix(spot_ref[0:1, :])
    own = y_ref[0]
    dq_sum = dq_in_ref[0, own].astype(F32)
    for y in range(1, NY):
        dq_sum = dq_sum + dq_in_ref[y, own].astype(F32)
    dq_sum = dq_sum.astype(BF)
    dq = dot(dq_sum[0:HD], place[0:CH])
    for c in range(1, NCH):
        dq = dq + dot(dq_sum[c * HD : (c + 1) * HD], place[c * CH : (c + 1) * CH])
    dq_ref[...] = dq.astype(BF)


VMEM = pl.BlockSpec(memory_space=pltpu.VMEM)
BLOCK = pl.BlockSpec()
SMEM = pl.BlockSpec(memory_space=pltpu.SMEM)
ANY = pl.BlockSpec(memory_space=pl.ANY)
MIB = 1024 * 1024


def call(kernel, name, outs, ins, out_spaces, scratch, flops, args, limit=8):
    return pl.pallas_call(
        kernel,
        out_shape=tuple(jax.ShapeDtypeStruct(s, d) for s, d in outs),
        in_specs=ins,
        out_specs=tuple(out_spaces),
        scratch_shapes=[pltpu.VMEM(*item) if isinstance(item, tuple) else item for item in scratch],
        compiler_params=pltpu.CompilerParams(vmem_limit_bytes=limit * MIB),
        cost_estimate=pl.CostEstimate(flops=flops, bytes_accessed=10**6, transcendentals=0),
        name=name,
    )(*args)


def prepare(count, keys, values, out_grad, keep):
    outs = [((NZ, TB + EXT, CH), BF), ((HD, TB), BF), ((8, TB), F32)]
    scratch = [((2 * HD, TB), BF), ((HD, TB), BF), ((TB,), jnp.int32), pltpu.SemaphoreType.DMA((4,))]
    args = (count, keys, values, out_grad, keep)
    return call(prepare_kernel, "prepare", outs, [SMEM] + [ANY] * 4, [VMEM] * 3, scratch, 10**8, args, 56)


def project(w_out, grad_all, queries, spot, after):
    outs = [((NY, 2 * HD + EXT, TB), BF)]
    args = (w_out, grad_all, queries, spot, after)
    return call(project_kernel, "project", outs, [BLOCK, VMEM, BLOCK, VMEM, ANY], [VMEM], [], 10**8, args)[0]


PACKED = [((KPAD, 2 * CH), BF), ((CH + EXT, KPAD), BF), ((2 * HD, QPAD), F32), ((2 * CH, QPAD), BF)]


def forward(kv_all, x_all):
    outs = [((NY, HD + 2 * EXT, TB), BF), ((32,), jnp.int32)]
    scratch = PACKED + [((HD, QPAD), F32), ((8, QPAD), F32)]
    args = (kv_all, x_all)
    return call(forward_kernel, "forward", outs, [VMEM] * 2, [VMEM, SMEM], scratch, 4 * 10**9, args, 20)


def combine(own, sc, got, grad_all, spot):
    outs = [((NY * NZ, HD, CH), BF)]
    args = (own, sc, got, grad_all, spot)
    return call(combine_kernel, "combine", outs, [SMEM] * 2 + [VMEM] * 3, [VMEM], [((8, QPAD), F32)], 10**8, args)[0]


def backward(kv_all, x_all, got):
    outs = [((NY, NCH * HD, CH), BF), ((NZ, TB + HD, CH), BF), ((32,), jnp.int32)]
    scratch = PACKED + [
        ((2 * CH, QPAD), BF),
        ((QPAD, CH), BF),
        ((QPAD, CH), BF),
        ((HD, QPAD), F32),
        ((KPAD, CH), F32),
    ]
    args = (kv_all, x_all, got)
    return call(backward_kernel, "backward", outs, [VMEM] * 3, [VMEM] * 2 + [SMEM], scratch, 8 * 10**9, args, 20)


def finish(got, dq_all, spot, own):
    outs = [((HD, TB), BF), ((HD, TB), BF), ((HD, TB), BF), ((HD, D), F32)]
    args = (own, got, dq_all, spot)
    return call(finish_kernel, "finish", outs, [SMEM] + [VMEM] * 3, [VMEM] * 4, [], 10**7, args)


def exchange(slots, axis, groups=None):
    return lax.all_to_all(slots, axis, 0, 0, tiled=True, axis_index_groups=groups)


def on_device(queries, keys, values, out_grad, w_out, counts, keep):
    kv, grad, spot = prepare(counts, keys, values, out_grad, keep)
    kv_all = exchange(kv, "tok", Z_GROUPS)
    grad_all = lax.all_gather(grad, "head", axis=0, tiled=True)
    x_all = exchange(project(w_out, grad_all, queries, spot, kv_all), "tok", Y_GROUPS)
    slots, sc = forward(kv_all, x_all)
    got = exchange(slots, "tok", Y_GROUPS)
    own = (lax.axis_index("tok") // NZ).astype(jnp.int32).reshape(1)
    parts = exchange(combine(own, sc, got, grad_all, spot), "tok")
    dq_parts, dkv_parts, _ = backward(kv_all, x_all, got)
    dq_all = lax.all_gather(dq_parts, "tok", axis=0, axis_index_groups=Y_GROUPS)
    piece = jnp.sum(parts.astype(F32), axis=0).astype(BF)
    dkv_parts = dkv_parts.at[:, TB:, :].set(piece[None])
    return finish(exchange(dkv_parts, "tok", Z_GROUPS), dq_all, spot, own)


def solution(mesh):
    return jax.shard_map(
        on_device,
        mesh=mesh,
        in_specs=(
            P("head", "tok"),
            P("head", "tok"),
            P("head", "tok"),
            P("head", "tok"),
            P("head", None),
            P("tok"),
            P("tok"),
        ),
        out_specs=(P("head", "tok"), P("head", "tok"), P("head", "tok"), P("head", None)),
        check_vma=False,
    )
```
